32 devices in a mesh: kv: 4 (over x, core), seq: 8 (over z, y).
Axes of the slice: x: 2, y: 2, z: 4, core: 2. Of those that a mesh axis runs over, the one named last changes fastest.
Arguments:
- hidden_states: bfloat16 [1536, 2048], P('seq')
- attn_gain: float32 [2048], replicated, may hold values from 0.5 to 1.5
- w_q: bfloat16 [2048, 2048], P(None, 'kv')
- w_k: bfloat16 [2048, 512], P(None, 'kv')
- w_v: bfloat16 [2048, 512], P(None, 'kv'), may hold values from -0.125 to 0.125
- w_o: bfloat16 [2048, 2048], P('kv'), may hold values from -0.125 to 0.125
- final_gain: float32 [2048], replicated, may hold values from 0.5 to 1.5
- w_head: bfloat16 [2048, 49408], P(None, ('kv', 'seq'))
- doc_lengths: int32 [8], replicated, may hold values from 1 to 768, as said below
- target_ids: int32 [1536], replicated, may hold values from 0 to 49154, as said below
- vocab_mask: int32 [49408], P(('kv', 'seq')), may hold values from 0 to 1, as said below
Outputs:
- log_probs: float32 [1536], P('seq')
- entropies: float32 [1536], P('seq')
The draws below stay inside these ranges and needn't reach their ends.
Inputs may be any that keep to these rules, and one draw needn't show every extreme that they name: `doc_lengths`: they sum to 1536; one is 768, one more is over 384, every other is under 64. `target_ids`: each names an entry whose vocab_mask is 1. `vocab_mask`: entries from 49155 on are 0.
All inputs are finite; a program needn't handle non-finite values.
Results may differ from the reference program's by a relative error of at most 0.0045.
Values may be sent and summed in bfloat16 or wider, within the bound.
A program may use at most 128 MiB of HBM per device.

```python
import math
import jax
import jax.numpy as jnp
from jax import lax

D = 2048
Q_HEADS = 32
KV_HEADS = 8
HEAD_DIM = 64
LIVE_VOCAB = 49155
TOK_DEV = 192
VOCAB = 49408
TOKENS = 1536
SHORTS = 6
DOCS = 8


def query_weight(key):
    return jax.random.normal(jax.random.fold_in(key, 211), (D, Q_HEADS * HEAD_DIM), jnp.float32) / math.sqrt(D)


def picked_columns(key):
    segment = LIVE_VOCAB // 6
    offsets = jax.random.randint(jax.random.fold_in(key, 231), (6,), 0, segment)
    return (jnp.arange(6, dtype=jnp.int32) * segment + offsets).astype(jnp.int32)


def vocab_tables(key):
    banned = jax.random.randint(jax.random.fold_in(key, 241), (VOCAB,), 0, 50) == 0
    vocab_index = jnp.arange(VOCAB, dtype=jnp.int32)
    live_table = ((vocab_index < LIVE_VOCAB) & jnp.logical_not(banned)).astype(jnp.int32)
    id_table = jax.random.randint(jax.random.fold_in(key, 242), (TOKENS,), 0, LIVE_VOCAB).astype(jnp.int32)
    spot_pos = jax.random.randint(jax.random.fold_in(key, 243), (), 0, TOKENS)
    id_table = id_table.at[spot_pos].set(LIVE_VOCAB - 1)
    id_table = id_table.at[(spot_pos + 1) % TOKENS].set(0)
    live_table = live_table.at[id_table].set(1)
    live_table = live_table.at[picked_columns(key)].set(1)
    return (live_table, id_table)


def draw_hidden_states(key, part):
    noise_part = jax.random.normal(jax.random.fold_in(key, 201), (TOKENS, D), jnp.float32)
    values = noise_part
    return values.astype(jnp.bfloat16)


def draw_w_q(key, part):
    return query_weight(key).astype(jnp.bfloat16)


def draw_w_k(key, part):
    noise_part = jax.random.normal(jax.random.fold_in(key, 212), (D, KV_HEADS * HEAD_DIM), jnp.float32) / math.sqrt(D)
    values = noise_part
    return values.astype(jnp.bfloat16)


def draw_w_head(key, part):
    base_part = jax.random.normal(jax.random.fold_in(key, 221), (D, VOCAB), jnp.float32) * (24.0 / math.sqrt(D))
    return base_part.astype(jnp.bfloat16)


def draw_doc_lengths(key, part):
    short_len = jax.random.randint(jax.random.fold_in(key, 251), (SHORTS,), 1, 64).astype(jnp.int32)
    long_one = jnp.full((1,), TOKENS // 2, jnp.int32)
    long_two = jnp.full((1,), TOKENS - TOKENS // 2, jnp.int32) - jnp.sum(short_len)
    all_lengths = jnp.concatenate([long_one, long_two.astype(jnp.int32), short_len])
    shuffle = jax.random.permutation(jax.random.fold_in(key, 252), DOCS)
    return all_lengths[shuffle].astype(jnp.int32)


def draw_target_ids(key, part):
    return vocab_tables(key)[1]


def draw_vocab_mask(key, part):
    return vocab_tables(key)[0]


def block_scale(stream_key, shape, cuts, low, top_value):
    def one(dim, parts):
        draws = jax.random.uniform(jax.random.fold_in(jax.random.fold_in(stream_key, 6), dim), (parts,), jnp.float32, low / len(cuts), top_value / len(cuts))
        return jnp.repeat(jnp.exp(draws), shape[dim] // parts).reshape((-1,) + (1,) * (len(shape) - dim - 1))

    level = one(*cuts[0])
    for cut in cuts[1:]:
        level = level * one(*cut)
    return level


def centred(own_key, dims, deviation, bound, cuts=(), held_as=jnp.bfloat16):
    values = jax.random.normal(own_key, dims, jnp.float32) * deviation
    if len(cuts) > 0:
        values = block_scale(own_key, dims, cuts, -0.22, 0.18) * values
    return jnp.clip(values, min=-bound, max=bound).astype(held_as)


def setup_inputs(seed: int = 0) -> dict:
    seeds = jax.random.split(jax.random.key(seed), 12)
    return {
        "hidden_states": draw_hidden_states(jax.random.fold_in(seeds[11], 71), 0),
        "attn_gain": jnp.clip(1.0 + 0.1 * jax.random.normal(seeds[1], (D,), jnp.float32), 0.5, 1.5),
        "w_q": draw_w_q(jax.random.fold_in(seeds[11], 71), 0),
        "w_k": draw_w_k(jax.random.fold_in(seeds[11], 71), 0),
        "w_v": centred(seeds[4], (D, KV_HEADS * HEAD_DIM), D ** -0.5, 0.125, ((1, 4),)),
        "w_o": centred(seeds[5], (Q_HEADS * HEAD_DIM, D), (Q_HEADS * HEAD_DIM) ** -0.5, 0.125, ((0, 4),)),
        "final_gain": jnp.clip(1.0 + 0.1 * jax.random.normal(seeds[6], (D,), jnp.float32), 0.5, 1.5),
        "w_head": draw_w_head(jax.random.fold_in(seeds[11], 71), 0),
        "doc_lengths": draw_doc_lengths(jax.random.fold_in(seeds[11], 71), 0),
        "target_ids": draw_target_ids(jax.random.fold_in(seeds[11], 71), 0),
        "vocab_mask": draw_vocab_mask(jax.random.fold_in(seeds[11], 71), 0),
    }


ROPE_THETA = 10000000.0
NORM_EPS = 1e-05
NEG_FILL = -1e+30
ATTN_SCALE = 0.015625
RESID_SCALE = 5.0
LOGIT_SCALE = 0.125

def rms_norm(values, gain_vec):
    return values * lax.rsqrt(lax.optimization_barrier(jnp.mean(values * values, axis=-1, keepdims=True)) + NORM_EPS) * gain_vec

def rotate(values, positions):
    half_dim = values.shape[-1] // 2
    inverse = jnp.exp(jnp.arange(half_dim, dtype=jnp.float32) * (-2.0 * math.log(ROPE_THETA) / values.shape[-1]))
    angles = positions.astype(jnp.float32)[:, None] * inverse[None, :]
    cos_val = jnp.cos(angles)[:, None, :]
    sine_val = jnp.sin(angles)[:, None, :]
    lower_half = values[..., :half_dim]
    upper_half = values[..., half_dim:]
    return jnp.concatenate([lower_half * cos_val - upper_half * sine_val, upper_half * cos_val + lower_half * sine_val], axis=-1)

def reference(hidden_states, attn_gain, w_q, w_k, w_v, w_o, final_gain, w_head, doc_lengths, target_ids, vocab_mask):
    stream = hidden_states.astype(jnp.float32)
    normed_in = rms_norm(stream, attn_gain).astype(jnp.bfloat16)
    queries = jnp.dot(normed_in, w_q, preferred_element_type=jnp.float32)
    key_proj = jnp.dot(normed_in, w_k, preferred_element_type=jnp.float32)
    value_proj = jnp.dot(normed_in, w_v, preferred_element_type=jnp.float32)
    doc_ends = jnp.cumsum(doc_lengths).astype(jnp.int32)
    doc_starts = (doc_ends - doc_lengths).astype(jnp.int32)
    token_pos = jnp.arange(TOKENS, dtype=jnp.int32)
    doc_start = lax.optimization_barrier(jnp.max(jnp.where(doc_starts[None, :] <= token_pos[:, None], doc_starts[None, :], 0), axis=1)).astype(jnp.int32)
    positions = token_pos - doc_start
    group_size = Q_HEADS // KV_HEADS
    rotated_q = rotate(queries.reshape(TOKENS, Q_HEADS, HEAD_DIM), positions).astype(jnp.bfloat16)
    rotated_q = rotated_q.reshape(TOKENS, KV_HEADS, group_size, HEAD_DIM)
    rotated_k = rotate(key_proj.reshape(TOKENS, KV_HEADS, HEAD_DIM), positions).astype(jnp.bfloat16)
    value_rows = value_proj.astype(jnp.bfloat16).reshape(TOKENS, KV_HEADS, HEAD_DIM)
    keys_f32 = rotated_k.astype(jnp.float32)
    values_f32 = value_rows.astype(jnp.float32)

    def attend(block_idx):
        row_first = (block_idx * TOK_DEV).astype(jnp.int32)
        q_block = lax.dynamic_slice_in_dim(rotated_q, row_first, TOK_DEV, 0).astype(jnp.float32)
        query_pos = row_first + jnp.arange(TOK_DEV, dtype=jnp.int32)
        query_start = lax.dynamic_slice_in_dim(doc_start, row_first, TOK_DEV, 0)
        scores = jnp.einsum('tkgd,skd->kgts', q_block, keys_f32) * ATTN_SCALE
        allowed = (token_pos[None, :] >= query_start[:, None]) & (token_pos[None, :] <= query_pos[:, None])
        scores = jnp.where(allowed, scores, NEG_FILL)
        top_score = lax.optimization_barrier(jnp.max(scores, axis=-1, keepdims=True))
        weights = jnp.where(allowed, jnp.exp(scores - top_score), 0.0)
        totals = lax.optimization_barrier(jnp.sum(weights, axis=-1))
        rounded = lax.optimization_barrier(weights.astype(jnp.bfloat16)).astype(jnp.float32)
        context = jnp.einsum('kgts,skd->kgtd', rounded, values_f32) / totals[..., None]
        return context.transpose(2, 0, 1, 3).reshape(TOK_DEV, Q_HEADS * HEAD_DIM).astype(jnp.bfloat16)
    context_all = lax.map(attend, jnp.arange(TOKENS // TOK_DEV, dtype=jnp.int32)).reshape(TOKENS, Q_HEADS * HEAD_DIM)
    attn_out = jnp.dot(context_all, w_o, preferred_element_type=jnp.float32)
    final_in = rms_norm(stream + RESID_SCALE * attn_out, final_gain).astype(jnp.bfloat16)
    live_mask = vocab_mask == 1

    def score(block_idx):
        row_first = (block_idx * TOK_DEV).astype(jnp.int32)
        rows = lax.dynamic_slice_in_dim(final_in, row_first, TOK_DEV, 0)
        row_ids = lax.dynamic_slice_in_dim(target_ids, row_first, TOK_DEV, 0)
        logits = jnp.dot(rows, w_head, preferred_element_type=jnp.float32) * LOGIT_SCALE
        masked = jnp.where(live_mask[None, :], logits, NEG_FILL)
        top_score = lax.optimization_barrier(jnp.max(masked, axis=1, keepdims=True))
        expw = jnp.where(live_mask[None, :], jnp.exp(masked - top_score), 0.0)
        totals = lax.optimization_barrier(jnp.sum(expw, axis=1, keepdims=True))
        log_total = top_score + jnp.log(totals)
        probs = expw / totals
        entropy = log_total[:, 0] - lax.optimization_barrier(jnp.sum(probs * jnp.where(live_mask[None, :], logits, 0.0), axis=1))
        target = jnp.take_along_axis(logits, row_ids[:, None].astype(jnp.int32), axis=1)[:, 0]
        return (target - log_total[:, 0], entropy)
    log_probs, entropies = lax.map(score, jnp.arange(TOKENS // TOK_DEV, dtype=jnp.int32))
    return (log_probs.reshape(TOKENS), entropies.reshape(TOKENS))
```

```python
import math

import jax
import jax.numpy as jnp
from jax import lax
from jax.sharding import PartitionSpec as P

HEAD_DIM = 64


ROPE_THETA = 10000000.0
NORM_EPS = 1e-05
NEG_FILL = -1e30
ATTN_SCALE = 0.015625
RESID_SCALE = 5.0
LOGIT_SCALE = 0.125


def rms_norm(values, gain_vec):
    return (
        values * lax.rsqrt(jnp.mean(values * values, axis=-1, keepdims=True) + NORM_EPS) * gain_vec
    )


def rotate(values, positions):
    half_dim = values.shape[-1] // 2
    inverse = jnp.exp(
        jnp.arange(half_dim, dtype=jnp.float32) * (-2.0 * math.log(ROPE_THETA) / values.shape[-1])
    )
    angles = positions.astype(jnp.float32)[:, None] * inverse[None, :]
    cos_val = jnp.cos(angles)[:, None, :]
    sine_val = jnp.sin(angles)[:, None, :]
    lower_half = values[..., :half_dim]
    upper_half = values[..., half_dim:]
    return jnp.concatenate(
        [
            lower_half * cos_val - upper_half * sine_val,
            upper_half * cos_val + lower_half * sine_val,
        ],
        axis=-1,
    )


def local(
    hidden_states,
    attn_gain,
    w_q,
    w_k,
    w_v,
    w_o,
    final_gain,
    w_head,
    doc_lengths,
    target_ids,
    vocab_mask,
):
    tok_rows = hidden_states.shape[0]
    seq_index = lax.axis_index("seq")
    kv_local = w_k.shape[1] // HEAD_DIM
    q_local = w_q.shape[1] // HEAD_DIM
    group_size = q_local // kv_local
    key_width = kv_local * HEAD_DIM
    stream = hidden_states.astype(jnp.float32)
    normed_in = rms_norm(stream, attn_gain).astype(jnp.bfloat16)
    queries = jnp.dot(normed_in, w_q, preferred_element_type=jnp.float32)
    key_proj = jnp.dot(normed_in, w_k, preferred_element_type=jnp.float32)
    value_proj = jnp.dot(normed_in, w_v, preferred_element_type=jnp.float32)
    token_pos = seq_index * tok_rows + jnp.arange(tok_rows, dtype=jnp.int32)
    docs = jnp.arange(doc_lengths.shape[0], dtype=jnp.int32)
    doc_starts = jnp.sum(jnp.where(docs[None, :] < docs[:, None], doc_lengths[None, :], 0), axis=1)
    doc_start = jnp.max(
        jnp.where(doc_starts[None, :] <= token_pos[:, None], doc_starts[None, :], 0), axis=1
    )
    positions = token_pos - doc_start
    rotated_q = rotate(queries.reshape(tok_rows, q_local, HEAD_DIM), positions).astype(jnp.bfloat16)
    rotated_q = rotated_q.reshape(tok_rows, kv_local, group_size, HEAD_DIM)
    rotated_k = rotate(key_proj.reshape(tok_rows, kv_local, HEAD_DIM), positions).astype(
        jnp.bfloat16
    )
    packed = jnp.concatenate(
        [rotated_k.reshape(tok_rows, key_width), value_proj.astype(jnp.bfloat16)], axis=1
    )
    earliest = doc_start[0]
    latest = token_pos[tok_rows - 1]
    initial = (
        jnp.full((kv_local, group_size, tok_rows), NEG_FILL, jnp.float32),
        jnp.zeros((kv_local, group_size, tok_rows), jnp.float32),
        jnp.zeros((kv_local, group_size, tok_rows, HEAD_DIM), jnp.float32),
    )
    shard_rows = lax.all_gather(packed, "seq", axis=0, tiled=True)
    offset = jnp.int32(0)
    row_count = shard_rows.shape[0]
    key_pos = jnp.arange(row_count, dtype=jnp.int32)

    def update(current):
        top_score, totals, context_sum = current
        key_rows = shard_rows[:, :key_width].reshape(row_count, kv_local, HEAD_DIM)
        value_rows = shard_rows[:, key_width:].reshape(row_count, kv_local, HEAD_DIM)
        scores = (
            jnp.einsum("tkgd,skd->kgts", rotated_q, key_rows, preferred_element_type=jnp.float32)
            * ATTN_SCALE
        )
        allowed = (key_pos[None, :] >= doc_start[:, None]) & (
            key_pos[None, :] <= token_pos[:, None]
        )
        scores = jnp.where(allowed, scores, NEG_FILL)
        new_top = jnp.maximum(top_score, jnp.max(scores, axis=-1))
        weights = jnp.where(allowed, jnp.exp(scores - new_top[..., None]), 0.0)
        rescale = jnp.exp(top_score - new_top)
        totals = jnp.sum(weights, axis=-1)
        context_sum = jnp.einsum(
            "kgts,skd->kgtd",
            weights.astype(jnp.bfloat16),
            value_rows,
            preferred_element_type=jnp.float32,
        )
        return (new_top, totals, context_sum)

    skip_piece = (offset + row_count <= earliest) | (offset > latest)
    top_score, totals, context_sum = lax.cond(skip_piece, lambda current: current, update, initial)
    context = (
        (context_sum / totals[..., None])
        .transpose(2, 0, 1, 3)
        .reshape(tok_rows, q_local * HEAD_DIM)
        .astype(jnp.bfloat16)
    )
    vocab_local = w_head.shape[1]
    flat_rank = lax.axis_index(("kv", "seq"))
    live_mask = vocab_mask == 1
    columns = flat_rank * vocab_local + jnp.arange(vocab_local, dtype=jnp.int32)
    attn_out = lax.psum(jnp.dot(context, w_o, preferred_element_type=jnp.float32), "kv")
    final_in = rms_norm(stream + RESID_SCALE * attn_out, final_gain).astype(jnp.bfloat16)
    head_shard_rows = lax.all_gather(final_in, "seq", axis=0, tiled=True)
    logits = jnp.dot(head_shard_rows, w_head, preferred_element_type=jnp.float32) * LOGIT_SCALE
    masked = jnp.where(live_mask[None, :], logits, NEG_FILL)
    top_row = jnp.max(masked, axis=1)
    shifted = jnp.where(live_mask[None, :], masked - top_row[:, None], 0.0)
    expw = jnp.where(live_mask[None, :], jnp.exp(shifted), 0.0)
    target = jnp.sum(jnp.where(target_ids[:, None] == columns[None, :], logits, 0.0), axis=1)
    row_stats = jnp.stack([top_row, jnp.sum(expw, axis=1), jnp.sum(expw * shifted, axis=1), target])
    top_all = lax.pmax(row_stats[0], ("kv", "seq"))
    rescale = jnp.exp(row_stats[0] - top_all)
    total_all, spread_all, target_all = lax.psum(
        (
            row_stats[1] * rescale,
            rescale * (row_stats[2] + (row_stats[0] - top_all) * row_stats[1]),
            row_stats[3],
        ),
        ("kv", "seq"),
    )
    log_prob = target_all - top_all - jnp.log(total_all)
    entropy = jnp.log(total_all) - spread_all / total_all
    log_probs = lax.dynamic_slice_in_dim(log_prob, seq_index * tok_rows, tok_rows, 0)
    entropies = lax.dynamic_slice_in_dim(entropy, seq_index * tok_rows, tok_rows, 0)
    return (log_probs, entropies)


def solution(mesh):
    in_specs = (
        P("seq", None),
        P(),
        P(None, "kv"),
        P(None, "kv"),
        P(None, "kv"),
        P("kv", None),
        P(),
        P(None, ("kv", "seq")),
        P(),
        P(),
        P(("kv", "seq")),
    )
    out_specs = (P("seq"), P("seq"))
    return jax.shard_map(local, mesh=mesh, in_specs=in_specs, out_specs=out_specs, check_vma=False)
```

```python
import functools
import math

import jax
import jax.numpy as jnp
from jax import lax
from jax.experimental import pallas as pl
from jax.experimental.pallas import tpu as pltpu
from jax.sharding import PartitionSpec as P

HEAD_DIM = 64


ROPE_THETA = 10000000.0
NORM_EPS = 1e-05
NEG_FILL = -1e30
ATTN_SCALE = 0.015625
RESID_SCALE = 5.0
LOGIT_SCALE = 0.125


def rms_norm(values, gain_vec):
    return (
        values * lax.rsqrt(jnp.mean(values * values, axis=-1, keepdims=True) + NORM_EPS) * gain_vec
    )


def rotate(values, positions):
    half_dim = values.shape[-1] // 2
    inverse = jnp.exp(
        jnp.arange(half_dim, dtype=jnp.float32) * (-2.0 * math.log(ROPE_THETA) / values.shape[-1])
    )
    angles = positions.astype(jnp.float32)[:, None] * inverse[None, :]
    cos_val = jnp.cos(angles)[:, None, :]
    sine_val = jnp.sin(angles)[:, None, :]
    lower_half = values[..., :half_dim]
    upper_half = values[..., half_dim:]
    return jnp.concatenate(
        [
            lower_half * cos_val - upper_half * sine_val,
            upper_half * cos_val + lower_half * sine_val,
        ],
        axis=-1,
    )


def enter(peers):
    barrier = pltpu.get_barrier_semaphore()
    for peer in peers:
        pl.semaphore_signal(barrier, inc=1, device_id=peer, device_id_type=pl.DeviceIdType.MESH)
    pl.semaphore_wait(barrier, len(peers))


def remote(src, dst, send_sem, recv_sem, peer):
    return pltpu.make_async_remote_copy(
        src_ref=src,
        dst_ref=dst,
        send_sem=send_sem,
        recv_sem=recv_sem,
        device_id=peer,
        device_id_type=pl.DeviceIdType.MESH,
    )


def seq_peer(kv_index, seq_index, step, seq_size):
    return {"kv": kv_index, "seq": lax.rem(seq_index + step, seq_size)}


def kv_peer(kv_index, seq_index, step, kv_size):
    return {"kv": lax.rem(kv_index + step, kv_size), "seq": seq_index}


def key_kernel(seq_size, reach, packed_ref, out_ref, local_sem, send_sem, recv_sem):
    kv_index, seq_index = lax.axis_index("kv"), lax.axis_index("seq")
    own = pltpu.make_async_copy(packed_ref, out_ref.at[reach], local_sem)
    own.start()
    enter([seq_peer(kv_index, seq_index, seq_size - d, seq_size) for d in range(1, reach + 1)])
    copies = []
    for d in range(1, reach + 1):
        copies.append(
            remote(
                packed_ref,
                out_ref.at[reach - d],
                send_sem.at[d - 1],
                recv_sem.at[d - 1],
                seq_peer(kv_index, seq_index, d, seq_size),
            )
        )
    for copy in copies:
        copy.start()
    own.wait()
    for copy in copies:
        copy.wait()


def gather_keys(packed, seq_size, reach):
    return pl.pallas_call(
        lambda *refs: key_kernel(seq_size, reach, *refs),
        out_shape=jax.ShapeDtypeStruct((reach + 1,) + packed.shape, packed.dtype),
        in_specs=[pl.BlockSpec(memory_space=pltpu.VMEM)],
        out_specs=pl.BlockSpec(memory_space=pltpu.VMEM),
        scratch_shapes=[
            pltpu.SemaphoreType.DMA,
            pltpu.SemaphoreType.DMA((reach,)),
            pltpu.SemaphoreType.DMA((reach,)),
        ],
        compiler_params=pltpu.CompilerParams(
            collective_id=0, has_side_effects=True, vmem_limit_bytes=40 * 2**20
        ),
    )(packed)


def block_plan(sizes, order):
    blocks = [(dict.fromkeys(order, 0), -1)]
    for level, dim in enumerate(order):
        fresh = []
        for place, _ in blocks:
            for step in range(1, sizes[dim]):
                fresh.append(({**place, dim: step}, level))
        blocks = blocks + fresh
    return blocks


def row_kernel(
    kv_size, seq_size, part_ref, hidden_ref, gain_ref, out_ref, heard, rs_send, rs_recv, send_sem, recv_sem
):
    kv_index, seq_index = lax.axis_index("kv"), lax.axis_index("seq")
    width = out_ref.shape[2]
    half = width // 2
    cores = 2 if kv_size % 2 == 0 else 1
    x_size = kv_size // cores
    y_size = x_size if seq_size % x_size == 0 else 1
    sizes = {"z": seq_size // y_size, "y": y_size, "x": x_size, "c": cores}
    mine = {
        "z": seq_index // y_size,
        "y": lax.rem(seq_index, y_size),
        "x": kv_index // cores,
        "c": lax.rem(kv_index, cores),
    }

    def at(place):
        now = {d: lax.rem(mine[d] + place[d], sizes[d]) if place[d] else mine[d] for d in sizes}
        return now["x"] * cores + now["c"], now["z"] * y_size + now["y"]

    def moved(dim, step):
        kv_at, seq_at = at({**dict.fromkeys(sizes, 0), dim: step})
        return {"kv": kv_at, "seq": seq_at}

    def slot(place):
        kv_at, seq_at = at(place)
        return seq_at * kv_size + kv_at

    peers = [kv_peer(kv_index, seq_index, step, kv_size) for step in range(1, kv_size)]
    peers += [moved(d, step) for d in ("z", "y") for step in range(1, sizes[d])]
    enter(peers)
    shares = []
    for step in range(1, kv_size):
        peer = kv_peer(kv_index, seq_index, step, kv_size)
        shares.append(
            remote(
                part_ref.at[peer["kv"]],
                heard.at[step - 1],
                rs_send.at[step - 1],
                rs_recv.at[step - 1],
                peer,
            )
        )
    for share in shares:
        share.start()
    total = part_ref[kv_index].astype(jnp.float32)
    for step, share in enumerate(shares):
        share.wait_recv()
        total = total + heard[step].astype(jnp.float32)
    values = hidden_ref[...].astype(jnp.float32) + RESID_SCALE * total
    out_ref[seq_index * kv_size + kv_index] = rms_norm(values, gain_ref[...]).astype(out_ref.dtype)

    orders = (("z", "y", "x", "c"), ("z", "x", "y", "c"))
    plans = [block_plan(sizes, order) for order in orders]
    sent = []
    used = [0, 0]
    for turn in range(kv_size * seq_size):
        for part in range(2):
            place, level = plans[part][turn]
            index = slot(place)
            view = out_ref.at[index, :, pl.ds(part * half, half)]
            if level >= 0:
                remote(
                    view, view, send_sem.at[part, 0], recv_sem.at[part, index], peers[0]
                ).wait_recv()
            for dim in orders[part][level + 1 :]:
                for step in range(1, sizes[dim]):
                    copy = remote(
                        view,
                        view,
                        send_sem.at[part, used[part]],
                        recv_sem.at[part, index],
                        moved(dim, step),
                    )
                    copy.start()
                    used[part] += 1
                    sent.append(copy)
    for copy in sent:
        copy.wait_send()
    for share in shares:
        share.wait_send()


def gather_rows(part, hidden, gain, kv_size, seq_size):
    _, rows, width = part.shape
    count = kv_size * seq_size
    return pl.pallas_call(
        lambda *refs: row_kernel(kv_size, seq_size, *refs),
        out_shape=jax.ShapeDtypeStruct((count, rows, width), jnp.bfloat16),
        in_specs=[pl.BlockSpec(memory_space=pltpu.VMEM)] * 3,
        out_specs=pl.BlockSpec(memory_space=pltpu.VMEM),
        scratch_shapes=[
            pltpu.VMEM((kv_size - 1, rows, width), jnp.bfloat16),
            pltpu.SemaphoreType.DMA((kv_size - 1,)),
            pltpu.SemaphoreType.DMA((kv_size - 1,)),
            pltpu.SemaphoreType.DMA((2, count)),
            pltpu.SemaphoreType.DMA((2, count)),
        ],
        compiler_params=pltpu.CompilerParams(
            collective_id=1, has_side_effects=True, vmem_limit_bytes=48 * 2**20
        ),
    )(part, hidden, gain)


def merge(stats):
    top = stats[0][0:1]
    for item in stats[1:]:
        top = jnp.maximum(top, item[0:1])
    total = spread = target = jnp.zeros_like(top)
    for item in stats:
        rescale = jnp.exp(item[0:1] - top)
        total = total + rescale * item[1:2]
        spread = spread + rescale * (item[2:3] + (item[0:1] - top) * item[1:2])
        target = target + item[3:4]
    return jnp.concatenate([top, total, spread, target], axis=0)


def stat_kernel(
    kv_size, seq_size, stat_ref, out_ref, near, block, far, send_one, recv_one, send_two, recv_two
):
    kv_index, seq_index = lax.axis_index("kv"), lax.axis_index("seq")
    by_seq = [seq_peer(kv_index, seq_index, step, seq_size) for step in range(1, seq_size)]
    by_kv = [kv_peer(kv_index, seq_index, step, kv_size) for step in range(1, kv_size)]
    enter(by_seq + by_kv)
    first = [
        remote(stat_ref.at[peer["seq"]], near.at[i], send_one.at[i], recv_one.at[i], peer)
        for i, peer in enumerate(by_seq)
    ]
    for copy in first:
        copy.start()
    for copy in first:
        copy.wait()
    block[...] = merge([stat_ref[seq_index]] + [near[i] for i in range(seq_size - 1)])
    second = [
        remote(block, far.at[i], send_two.at[i], recv_two.at[i], peer)
        for i, peer in enumerate(by_kv)
    ]
    for copy in second:
        copy.start()
    for copy in second:
        copy.wait()
    out_ref[...] = merge([block[...]] + [far[i] for i in range(kv_size - 1)])


def merge_stats(stats, kv_size, seq_size):
    one = stats.shape[1:]
    return pl.pallas_call(
        lambda *refs: stat_kernel(kv_size, seq_size, *refs),
        out_shape=jax.ShapeDtypeStruct(one, jnp.float32),
        in_specs=[pl.BlockSpec(memory_space=pltpu.VMEM)],
        out_specs=pl.BlockSpec(memory_space=pltpu.VMEM),
        scratch_shapes=[
            pltpu.VMEM((seq_size - 1,) + one, jnp.float32),
            pltpu.VMEM(one, jnp.float32),
            pltpu.VMEM((kv_size - 1,) + one, jnp.float32),
            pltpu.SemaphoreType.DMA((seq_size - 1,)),
            pltpu.SemaphoreType.DMA((seq_size - 1,)),
            pltpu.SemaphoreType.DMA((kv_size - 1,)),
            pltpu.SemaphoreType.DMA((kv_size - 1,)),
        ],
        compiler_params=pltpu.CompilerParams(
            collective_id=2, has_side_effects=True, vmem_limit_bytes=32 * 2**20
        ),
    )(stats)


def local(
    kv_size,
    seq_size,
    hidden_states,
    attn_gain,
    w_q,
    w_k,
    w_v,
    w_o,
    final_gain,
    w_head,
    doc_lengths,
    target_ids,
    vocab_mask,
):
    tok_rows = hidden_states.shape[0]
    seq_index = lax.axis_index("seq")
    kv_local = w_k.shape[1] // HEAD_DIM
    q_local = w_q.shape[1] // HEAD_DIM
    group_size = q_local // kv_local
    key_width = kv_local * HEAD_DIM
    stream = hidden_states.astype(jnp.float32)
    normed_in = rms_norm(stream, attn_gain).astype(jnp.bfloat16)
    queries = jnp.dot(normed_in, w_q, preferred_element_type=jnp.float32)
    key_proj = jnp.dot(normed_in, w_k, preferred_element_type=jnp.float32)
    value_proj = jnp.dot(normed_in, w_v, preferred_element_type=jnp.float32)
    token_pos = seq_index * tok_rows + jnp.arange(tok_rows, dtype=jnp.int32)
    docs = jnp.arange(doc_lengths.shape[0], dtype=jnp.int32)
    doc_starts = jnp.sum(jnp.where(docs[None, :] < docs[:, None], doc_lengths[None, :], 0), axis=1)
    doc_start = jnp.max(
        jnp.where(doc_starts[None, :] <= token_pos[:, None], doc_starts[None, :], 0), axis=1
    )
    positions = token_pos - doc_start
    rotated_q = rotate(queries.reshape(tok_rows, q_local, HEAD_DIM), positions).astype(jnp.bfloat16)
    rotated_q = rotated_q.reshape(tok_rows, kv_local, group_size, HEAD_DIM)
    rotated_k = rotate(key_proj.reshape(tok_rows, kv_local, HEAD_DIM), positions).astype(
        jnp.bfloat16
    )
    packed = jnp.concatenate(
        [rotated_k.reshape(tok_rows, key_width), value_proj.astype(jnp.bfloat16)], axis=1
    )
    reach = (seq_size + 1) // 2
    key_blocks = gather_keys(packed, seq_size, reach)
    row_count = (reach + 1) * tok_rows
    shard_rows = key_blocks.reshape(row_count, 2 * key_width)
    key_pos = (seq_index - reach) * tok_rows + jnp.arange(row_count, dtype=jnp.int32)
    key_rows = shard_rows[:, :key_width].reshape(row_count, kv_local, HEAD_DIM)
    value_rows = shard_rows[:, key_width:].reshape(row_count, kv_local, HEAD_DIM)
    scores = (
        jnp.einsum("tkgd,skd->kgts", rotated_q, key_rows, preferred_element_type=jnp.float32)
        * ATTN_SCALE
    )
    allowed = (key_pos[None, :] >= doc_start[:, None]) & (key_pos[None, :] <= token_pos[:, None])
    scores = jnp.where(allowed, scores, NEG_FILL)
    top_score = jnp.max(scores, axis=-1)
    weights = jnp.where(allowed, jnp.exp(scores - top_score[..., None]), 0.0)
    totals = jnp.sum(weights, axis=-1)
    context_sum = jnp.einsum(
        "kgts,skd->kgtd",
        weights.astype(jnp.bfloat16),
        value_rows,
        preferred_element_type=jnp.float32,
    )
    context = (
        (context_sum / totals[..., None])
        .transpose(2, 0, 1, 3)
        .reshape(tok_rows, q_local * HEAD_DIM)
        .astype(jnp.bfloat16)
    )
    vocab_local = w_head.shape[1]
    flat_rank = lax.axis_index(("kv", "seq"))
    live_mask = vocab_mask == 1
    columns = flat_rank * vocab_local + jnp.arange(vocab_local, dtype=jnp.int32)
    own_rows = tok_rows // kv_size
    part = jnp.dot(context, w_o, preferred_element_type=jnp.float32).astype(jnp.bfloat16)
    own_hidden = lax.dynamic_slice_in_dim(
        hidden_states, lax.axis_index("kv") * own_rows, own_rows, 0
    )
    head_shard_rows = gather_rows(
        part.reshape(kv_size, own_rows, part.shape[1]),
        own_hidden,
        final_gain[None, :],
        kv_size,
        seq_size,
    ).reshape(tok_rows * seq_size, part.shape[1])
    logits = jnp.dot(head_shard_rows, w_head, preferred_element_type=jnp.float32) * LOGIT_SCALE
    masked = jnp.where(live_mask[None, :], logits, NEG_FILL)
    top_row = jnp.max(masked, axis=1)
    shifted = jnp.where(live_mask[None, :], masked - top_row[:, None], 0.0)
    expw = jnp.where(live_mask[None, :], jnp.exp(shifted), 0.0)
    target = jnp.sum(jnp.where(target_ids[:, None] == columns[None, :], logits, 0.0), axis=1)
    row_stats = jnp.stack([top_row, jnp.sum(expw, axis=1), jnp.sum(expw * shifted, axis=1), target])
    blocks = row_stats.reshape(4, seq_size, tok_rows).transpose(1, 0, 2)
    top_all, total_all, spread_all, target_all = merge_stats(blocks, kv_size, seq_size)
    log_probs = target_all - top_all - jnp.log(total_all)
    entropies = jnp.log(total_all) - spread_all / total_all
    return (log_probs, entropies)


def solution(mesh):
    in_specs = (
        P("seq", None),
        P(),
        P(None, "kv"),
        P(None, "kv"),
        P(None, "kv"),
        P("kv", None),
        P(),
        P(None, ("kv", "seq")),
        P(),
        P(),
        P(("kv", "seq")),
    )
    out_specs = (P("seq"), P("seq"))
    sizes = (mesh.shape["kv"], mesh.shape["seq"])
    return jax.shard_map(functools.partial(local, *sizes), mesh=mesh, in_specs=in_specs, out_specs=out_specs, check_vma=False)
```

```python
import functools
import math

import jax
import jax.numpy as jnp
from jax import lax
from jax.experimental import pallas as pl
from jax.experimental.pallas import tpu as pltpu
from jax.sharding import PartitionSpec as P

HEAD_DIM = 64


ROPE_THETA = 10000000.0
NORM_EPS = 1e-05
NEG_FILL = -1e30
ATTN_SCALE = 0.015625
RESID_SCALE = 5.0
LOGIT_SCALE = 0.125


def rms_norm(values, gain_vec):
    return (
        values * lax.rsqrt(jnp.mean(values * values, axis=-1, keepdims=True) + NORM_EPS) * gain_vec
    )


def rotate(values, positions):
    half_dim = values.shape[-1] // 2
    inverse = jnp.exp(
        jnp.arange(half_dim, dtype=jnp.float32) * (-2.0 * math.log(ROPE_THETA) / values.shape[-1])
    )
    angles = positions.astype(jnp.float32)[:, None] * inverse[None, :]
    cos_val = jnp.cos(angles)[:, None, :]
    sine_val = jnp.sin(angles)[:, None, :]
    lower_half = values[..., :half_dim]
    upper_half = values[..., half_dim:]
    return jnp.concatenate(
        [
            lower_half * cos_val - upper_half * sine_val,
            upper_half * cos_val + lower_half * sine_val,
        ],
        axis=-1,
    )


def enter(peers):
    barrier = pltpu.get_barrier_semaphore()
    for peer in peers:
        pl.semaphore_signal(barrier, inc=1, device_id=peer, device_id_type=pl.DeviceIdType.MESH)
    pl.semaphore_wait(barrier, len(peers))


def remote(src, dst, send_sem, recv_sem, peer):
    return pltpu.make_async_remote_copy(
        src_ref=src,
        dst_ref=dst,
        send_sem=send_sem,
        recv_sem=recv_sem,
        device_id=peer,
        device_id_type=pl.DeviceIdType.MESH,
    )


def seq_peer(kv_index, seq_index, step, seq_size):
    return {"kv": kv_index, "seq": lax.rem(seq_index + step, seq_size)}


def kv_peer(kv_index, seq_index, step, kv_size):
    return {"kv": lax.rem(kv_index + step, kv_size), "seq": seq_index}


def key_kernel(seq_size, reach, packed_ref, out_ref, local_sem, send_sem, recv_sem):
    kv_index, seq_index = lax.axis_index("kv"), lax.axis_index("seq")
    own = pltpu.make_async_copy(packed_ref, out_ref.at[reach], local_sem)
    own.start()
    enter([seq_peer(kv_index, seq_index, seq_size - d, seq_size) for d in range(1, reach + 1)])
    copies = []
    for d in range(1, reach + 1):
        copies.append(
            remote(
                packed_ref,
                out_ref.at[reach - d],
                send_sem.at[d - 1],
                recv_sem.at[d - 1],
                seq_peer(kv_index, seq_index, d, seq_size),
            )
        )
    for copy in copies:
        copy.start()
    own.wait()
    for copy in copies:
        copy.wait()


def gather_keys(packed, seq_size, reach):
    return pl.pallas_call(
        lambda *refs: key_kernel(seq_size, reach, *refs),
        out_shape=jax.ShapeDtypeStruct((reach + 1,) + packed.shape, packed.dtype),
        in_specs=[pl.BlockSpec(memory_space=pltpu.VMEM)],
        out_specs=pl.BlockSpec(memory_space=pltpu.VMEM),
        scratch_shapes=[
            pltpu.SemaphoreType.DMA,
            pltpu.SemaphoreType.DMA((reach,)),
            pltpu.SemaphoreType.DMA((reach,)),
        ],
        compiler_params=pltpu.CompilerParams(
            collective_id=0, has_side_effects=True, vmem_limit_bytes=40 * 2**20
        ),
    )(packed)


def block_plan(sizes, order):
    blocks = [(dict.fromkeys(order, 0), -1)]
    for level, dim in enumerate(order):
        fresh = []
        for place, _ in blocks:
            for step in range(1, sizes[dim]):
                fresh.append(({**place, dim: step}, level))
        blocks = blocks + fresh
    return blocks


def row_kernel(
    kv_size, seq_size, part_ref, hidden_ref, gain_ref, out_ref, heard, rs_send, rs_recv, send_sem, recv_sem
):
    kv_index, seq_index = lax.axis_index("kv"), lax.axis_index("seq")
    width = out_ref.shape[2]
    half = width // 2
    cores = 2 if kv_size % 2 == 0 else 1
    x_size = kv_size // cores
    y_size = x_size if seq_size % x_size == 0 else 1
    sizes = {"z": seq_size // y_size, "y": y_size, "x": x_size, "c": cores}
    mine = {
        "z": seq_index // y_size,
        "y": lax.rem(seq_index, y_size),
        "x": kv_index // cores,
        "c": lax.rem(kv_index, cores),
    }

    def at(place):
        now = {d: lax.rem(mine[d] + place[d], sizes[d]) if place[d] else mine[d] for d in sizes}
        return now["x"] * cores + now["c"], now["z"] * y_size + now["y"]

    def moved(dim, step):
        kv_at, seq_at = at({**dict.fromkeys(sizes, 0), dim: step})
        return {"kv": kv_at, "seq": seq_at}

    def slot(place):
        kv_at, seq_at = at(place)
        return seq_at * kv_size + kv_at

    peers = [kv_peer(kv_index, seq_index, step, kv_size) for step in range(1, kv_size)]
    peers += [moved(d, step) for d in ("z", "y") for step in range(1, sizes[d])]
    enter(peers)
    shares = []
    for step in range(1, kv_size):
        peer = kv_peer(kv_index, seq_index, step, kv_size)
        shares.append(
            remote(
                part_ref.at[peer["kv"]],
                heard.at[step - 1],
                rs_send.at[step - 1],
                rs_recv.at[step - 1],
                peer,
            )
        )
    for share in shares:
        share.start()
    total = part_ref[kv_index].astype(jnp.float32)
    for step, share in enumerate(shares):
        share.wait_recv()
        total = total + heard[step].astype(jnp.float32)
    values = hidden_ref[...].astype(jnp.float32) + RESID_SCALE * total
    out_ref[seq_index * kv_size + kv_index] = rms_norm(values, gain_ref[...]).astype(out_ref.dtype)

    orders = (("z", "y", "x", "c"), ("z", "x", "y", "c"))
    plans = [block_plan(sizes, order) for order in orders]
    sent = []
    used = [0, 0]
    for turn in range(kv_size * seq_size):
        for part in range(2):
            place, level = plans[part][turn]
            index = slot(place)
            view = out_ref.at[index, :, pl.ds(part * half, half)]
            if level >= 0:
                remote(
                    view, view, send_sem.at[part, 0], recv_sem.at[part, index], peers[0]
                ).wait_recv()
            for dim in orders[part][level + 1 :]:
                for step in range(1, sizes[dim]):
                    copy = remote(
                        view,
                        view,
                        send_sem.at[part, used[part]],
                        recv_sem.at[part, index],
                        moved(dim, step),
                    )
                    copy.start()
                    used[part] += 1
                    sent.append(copy)
    for copy in sent:
        copy.wait_send()
    for share in shares:
        share.wait_send()


def head_kernel(
    kv_size,
    seq_size,
    part_ref,
    hidden_ref,
    gain_ref,
    target_ref,
    live_ref,
    column_ref,
    head_ref,
    stat_ref,
    held,
    head,
    scored,
    heard,
    head_sem,
    rs_send,
    rs_recv,
    send_sem,
    recv_sem,
):
    kv_index, seq_index = lax.axis_index("kv"), lax.axis_index("seq")
    width = held.shape[2]
    half = width // 2
    rows = held.shape[1]
    weights = pltpu.make_async_copy(head_ref, head, head_sem)
    weights.start()
    cores = 2 if kv_size % 2 == 0 else 1
    x_size = kv_size // cores
    y_size = x_size if seq_size % x_size == 0 else 1
    sizes = {"z": seq_size // y_size, "y": y_size, "x": x_size, "c": cores}
    mine = {
        "z": seq_index // y_size,
        "y": lax.rem(seq_index, y_size),
        "x": kv_index // cores,
        "c": lax.rem(kv_index, cores),
    }

    def at(place):
        now = {d: lax.rem(mine[d] + place[d], sizes[d]) if place[d] else mine[d] for d in sizes}
        return now["x"] * cores + now["c"], now["z"] * y_size + now["y"]

    def moved(dim, step):
        kv_at, seq_at = at({**dict.fromkeys(sizes, 0), dim: step})
        return {"kv": kv_at, "seq": seq_at}

    def slot(place):
        kv_at, seq_at = at(place)
        column = (kv_at // cores) * y_size + lax.rem(seq_at, y_size)
        return (column * sizes["z"] + seq_at // y_size) * cores + lax.rem(kv_at, cores)

    peers = [kv_peer(kv_index, seq_index, step, kv_size) for step in range(1, kv_size)]
    peers += [moved(d, step) for d in ("z", "y") for step in range(1, sizes[d])]
    enter(peers)
    shares = []
    for step in range(1, kv_size):
        peer = kv_peer(kv_index, seq_index, step, kv_size)
        shares.append(
            remote(
                part_ref.at[peer["kv"]],
                heard.at[step - 1],
                rs_send.at[step - 1],
                rs_recv.at[step - 1],
                peer,
            )
        )
    for share in shares:
        share.start()
    total = part_ref[kv_index].astype(jnp.float32)
    for step, share in enumerate(shares):
        share.wait_recv()
        total = total + heard[step].astype(jnp.float32)
    values = hidden_ref[...].astype(jnp.float32) + RESID_SCALE * total
    held[slot(dict.fromkeys(sizes, 0))] = rms_norm(values, gain_ref[...]).astype(held.dtype)

    orders = (("z", "y", "x", "c"), ("z", "x", "y", "c"))
    sent = []
    used = [0, 0]

    def arrive(part, place):
        index = slot(place)
        view = held.at[index, :, pl.ds(part * half, half)]
        level = max([n for n, dim in enumerate(orders[part]) if place[dim]], default=-1)
        if level >= 0:
            remote(
                view, view, send_sem.at[part, 0], recv_sem.at[part, index], peers[0]
            ).wait_recv()
        for dim in orders[part][level + 1 :]:
            for step in range(1, sizes[dim]):
                copy = remote(
                    view,
                    view,
                    send_sem.at[part, used[part]],
                    recv_sem.at[part, index],
                    moved(dim, step),
                )
                copy.start()
                used[part] += 1
                sent.append(copy)

    depth = sizes["z"] * cores
    high = depth * rows
    total_columns = head.shape[1]
    cuts = [*range(0, total_columns - 511, 512)]
    tiles = list(zip(cuts, cuts[1:] + [total_columns])) if cuts else [(0, total_columns)]

    def score(x_step, y_step):
        first = slot({"z": 0, "y": y_step, "x": x_step, "c": 0}) // depth
        block = held[pl.ds(first * depth, depth)].reshape(high, width)
        wanted = jnp.broadcast_to(target_ref[first], (128, high)).T[:, 0:1]
        top = jnp.full((high, 1), NEG_FILL, jnp.float32)
        target = jnp.zeros((high, 1), jnp.float32)
        for low, end in tiles:
            logits = (
                jnp.dot(block, head[:, low:end], preferred_element_type=jnp.float32) * LOGIT_SCALE
            )
            masked = jnp.where(live_ref[:, low:end] == 1, logits, NEG_FILL)
            scored[:, low:end] = masked
            top = jnp.maximum(top, jnp.max(masked, axis=1, keepdims=True))
            hit = column_ref[:, low:end] == wanted
            target = target + jnp.sum(jnp.where(hit, logits, 0.0), axis=1, keepdims=True)
        total = jnp.zeros((high, 1), jnp.float32)
        spread = jnp.zeros((high, 1), jnp.float32)
        for low, end in tiles:
            shifted = scored[:, low:end] - top
            expw = jnp.exp(shifted)
            total = total + jnp.sum(expw, axis=1, keepdims=True)
            spread = spread + jnp.sum(expw * shifted, axis=1, keepdims=True)
        lane = lax.broadcasted_iota(jnp.int32, (high, 128), 1)
        table = jnp.where(lane == 0, top, jnp.where(lane == 1, total, jnp.where(lane == 2, spread, target)))
        stat_ref[first] = table.T[0:8]

    spots = [(i, j) for i in range(x_size) for j in range(y_size)]
    for stage in range(3):
        now = [spot for spot in spots if (spot[0] > 0) + (spot[1] > 0) == stage]
        for z_step in range(sizes["z"]):
            for i, j in now:
                for part in range(2):
                    arrive(part, {"z": z_step, "y": j, "x": i, "c": 0})
        if stage == 0:
            weights.wait()
        for i, j in now:
            for z_step in range(sizes["z"]):
                for c_step in range(1, cores):
                    for part in range(2):
                        arrive(part, {"z": z_step, "y": j, "x": i, "c": c_step})
            score(i, j)
    for copy in sent:
        copy.wait_send()
    for share in shares:
        share.wait_send()


def split_of(kv_size, seq_size):
    cores = 2 if kv_size % 2 == 0 else 1
    x_size = kv_size // cores
    y_size = x_size if seq_size % x_size == 0 else 1
    return seq_size // y_size, y_size, x_size, cores


def score_rows(part, hidden, gain, target_ids, live, columns, head, kv_size, seq_size):
    _, rows, width = part.shape
    count = kv_size * seq_size
    z_size, y_size, x_size, cores = split_of(kv_size, seq_size)
    spots = x_size * y_size
    high = z_size * cores * rows
    targets = target_ids.reshape(z_size, y_size, x_size, cores * rows)
    targets = targets.transpose(2, 1, 0, 3).reshape(spots, 1, high)
    stats = pl.pallas_call(
        lambda *refs: head_kernel(kv_size, seq_size, *refs),
        out_shape=jax.ShapeDtypeStruct((spots, 8, high), jnp.float32),
        in_specs=[pl.BlockSpec(memory_space=pltpu.VMEM)] * 6
        + [pl.BlockSpec(memory_space=pl.ANY)],
        out_specs=pl.BlockSpec(memory_space=pltpu.VMEM),
        scratch_shapes=[
            pltpu.VMEM((count, rows, width), jnp.bfloat16),
            pltpu.VMEM(head.shape, jnp.bfloat16),
            pltpu.VMEM((high, head.shape[1]), jnp.float32),
            pltpu.VMEM((kv_size - 1, rows, width), jnp.bfloat16),
            pltpu.SemaphoreType.DMA,
            pltpu.SemaphoreType.DMA((kv_size - 1,)),
            pltpu.SemaphoreType.DMA((kv_size - 1,)),
            pltpu.SemaphoreType.DMA((2, count)),
            pltpu.SemaphoreType.DMA((2, count)),
        ],
        compiler_params=pltpu.CompilerParams(
            collective_id=3, has_side_effects=True, vmem_limit_bytes=48 * 2**20
        ),
    )(part, hidden, gain, targets, live, columns, head)
    stats = stats[:, :4].reshape(x_size, y_size, 4, z_size, cores * rows)
    return stats.transpose(3, 1, 2, 0, 4).reshape(seq_size, 4, kv_size * rows)


def gather_rows(part, hidden, gain, kv_size, seq_size):
    _, rows, width = part.shape
    count = kv_size * seq_size
    return pl.pallas_call(
        lambda *refs: row_kernel(kv_size, seq_size, *refs),
        out_shape=jax.ShapeDtypeStruct((count, rows, width), jnp.bfloat16),
        in_specs=[pl.BlockSpec(memory_space=pltpu.VMEM)] * 3,
        out_specs=pl.BlockSpec(memory_space=pltpu.VMEM),
        scratch_shapes=[
            pltpu.VMEM((kv_size - 1, rows, width), jnp.bfloat16),
            pltpu.SemaphoreType.DMA((kv_size - 1,)),
            pltpu.SemaphoreType.DMA((kv_size - 1,)),
            pltpu.SemaphoreType.DMA((2, count)),
            pltpu.SemaphoreType.DMA((2, count)),
        ],
        compiler_params=pltpu.CompilerParams(
            collective_id=1, has_side_effects=True, vmem_limit_bytes=48 * 2**20
        ),
    )(part, hidden, gain)


def merge(stats):
    top = stats[0][0:1]
    for item in stats[1:]:
        top = jnp.maximum(top, item[0:1])
    total = spread = target = jnp.zeros_like(top)
    for item in stats:
        rescale = jnp.exp(item[0:1] - top)
        total = total + rescale * item[1:2]
        spread = spread + rescale * (item[2:3] + (item[0:1] - top) * item[1:2])
        target = target + item[3:4]
    return jnp.concatenate([top, total, spread, target], axis=0)


def stat_kernel(
    kv_size, seq_size, stat_ref, out_ref, near, block, far, send_one, recv_one, send_two, recv_two
):
    kv_index, seq_index = lax.axis_index("kv"), lax.axis_index("seq")
    by_seq = [seq_peer(kv_index, seq_index, step, seq_size) for step in range(1, seq_size)]
    by_kv = [kv_peer(kv_index, seq_index, step, kv_size) for step in range(1, kv_size)]
    enter(by_seq + by_kv)
    first = [
        remote(stat_ref.at[peer["seq"]], near.at[i], send_one.at[i], recv_one.at[i], peer)
        for i, peer in enumerate(by_seq)
    ]
    for copy in first:
        copy.start()
    for copy in first:
        copy.wait()
    block[...] = merge([stat_ref[seq_index]] + [near[i] for i in range(seq_size - 1)])
    second = [
        remote(block, far.at[i], send_two.at[i], recv_two.at[i], peer)
        for i, peer in enumerate(by_kv)
    ]
    for copy in second:
        copy.start()
    for copy in second:
        copy.wait()
    out_ref[...] = merge([block[...]] + [far[i] for i in range(kv_size - 1)])


def merge_stats(stats, kv_size, seq_size):
    one = stats.shape[1:]
    return pl.pallas_call(
        lambda *refs: stat_kernel(kv_size, seq_size, *refs),
        out_shape=jax.ShapeDtypeStruct(one, jnp.float32),
        in_specs=[pl.BlockSpec(memory_space=pltpu.VMEM)],
        out_specs=pl.BlockSpec(memory_space=pltpu.VMEM),
        scratch_shapes=[
            pltpu.VMEM((seq_size - 1,) + one, jnp.float32),
            pltpu.VMEM(one, jnp.float32),
            pltpu.VMEM((kv_size - 1,) + one, jnp.float32),
            pltpu.SemaphoreType.DMA((seq_size - 1,)),
            pltpu.SemaphoreType.DMA((seq_size - 1,)),
            pltpu.SemaphoreType.DMA((kv_size - 1,)),
            pltpu.SemaphoreType.DMA((kv_size - 1,)),
        ],
        compiler_params=pltpu.CompilerParams(
            collective_id=2, has_side_effects=True, vmem_limit_bytes=32 * 2**20
        ),
    )(stats)


def local(
    kv_size,
    seq_size,
    hidden_states,
    attn_gain,
    w_q,
    w_k,
    w_v,
    w_o,
    final_gain,
    w_head,
    doc_lengths,
    target_ids,
    vocab_mask,
):
    tok_rows = hidden_states.shape[0]
    seq_index = lax.axis_index("seq")
    kv_local = w_k.shape[1] // HEAD_DIM
    q_local = w_q.shape[1] // HEAD_DIM
    group_size = q_local // kv_local
    key_width = kv_local * HEAD_DIM
    stream = hidden_states.astype(jnp.float32)
    normed_in = rms_norm(stream, attn_gain).astype(jnp.bfloat16)
    queries = jnp.dot(normed_in, w_q, preferred_element_type=jnp.float32)
    key_proj = jnp.dot(normed_in, w_k, preferred_element_type=jnp.float32)
    value_proj = jnp.dot(normed_in, w_v, preferred_element_type=jnp.float32)
    token_pos = seq_index * tok_rows + jnp.arange(tok_rows, dtype=jnp.int32)
    docs = jnp.arange(doc_lengths.shape[0], dtype=jnp.int32)
    doc_starts = jnp.sum(jnp.where(docs[None, :] < docs[:, None], doc_lengths[None, :], 0), axis=1)
    doc_start = jnp.max(
        jnp.where(doc_starts[None, :] <= token_pos[:, None], doc_starts[None, :], 0), axis=1
    )
    positions = token_pos - doc_start
    rotated_q = rotate(queries.reshape(tok_rows, q_local, HEAD_DIM), positions).astype(jnp.bfloat16)
    rotated_q = rotated_q.reshape(tok_rows, kv_local, group_size, HEAD_DIM)
    rotated_k = rotate(key_proj.reshape(tok_rows, kv_local, HEAD_DIM), positions).astype(
        jnp.bfloat16
    )
    packed = jnp.concatenate(
        [rotated_k.reshape(tok_rows, key_width), value_proj.astype(jnp.bfloat16)], axis=1
    )
    reach = (seq_size + 1) // 2
    key_blocks = gather_keys(packed, seq_size, reach)
    row_count = (reach + 1) * tok_rows
    shard_rows = key_blocks.reshape(row_count, 2 * key_width)
    key_pos = (seq_index - reach) * tok_rows + jnp.arange(row_count, dtype=jnp.int32)
    key_rows = shard_rows[:, :key_width].reshape(row_count, kv_local, HEAD_DIM)
    value_rows = shard_rows[:, key_width:].reshape(row_count, kv_local, HEAD_DIM)
    scores = (
        jnp.einsum("tkgd,skd->kgts", rotated_q, key_rows, preferred_element_type=jnp.float32)
        * ATTN_SCALE
    )
    allowed = (key_pos[None, :] >= doc_start[:, None]) & (key_pos[None, :] <= token_pos[:, None])
    scores = jnp.where(allowed, scores, NEG_FILL)
    top_score = jnp.max(scores, axis=-1)
    weights = jnp.where(allowed, jnp.exp(scores - top_score[..., None]), 0.0)
    totals = jnp.sum(weights, axis=-1)
    context_sum = jnp.einsum(
        "kgts,skd->kgtd",
        weights.astype(jnp.bfloat16),
        value_rows,
        preferred_element_type=jnp.float32,
    )
    context = (
        (context_sum / totals[..., None])
        .transpose(2, 0, 1, 3)
        .reshape(tok_rows, q_local * HEAD_DIM)
        .astype(jnp.bfloat16)
    )
    vocab_local = w_head.shape[1]
    flat_rank = lax.axis_index(("kv", "seq"))
    live_mask = vocab_mask == 1
    columns = flat_rank * vocab_local + jnp.arange(vocab_local, dtype=jnp.int32)
    own_rows = tok_rows // kv_size
    part = jnp.dot(context, w_o, preferred_element_type=jnp.float32).astype(jnp.bfloat16)
    own_hidden = lax.dynamic_slice_in_dim(
        hidden_states, lax.axis_index("kv") * own_rows, own_rows, 0
    )
    if own_rows % 16 == 0:
        blocks = score_rows(
            part.reshape(kv_size, own_rows, part.shape[1]),
            own_hidden,
            final_gain[None, :],
            target_ids,
            vocab_mask[None, :],
            columns[None, :],
            w_head,
            kv_size,
            seq_size,
        )
    else:
        head_shard_rows = gather_rows(
            part.reshape(kv_size, own_rows, part.shape[1]),
            own_hidden,
            final_gain[None, :],
            kv_size,
            seq_size,
        ).reshape(tok_rows * seq_size, part.shape[1])
        logits = jnp.dot(head_shard_rows, w_head, preferred_element_type=jnp.float32) * LOGIT_SCALE
        masked = jnp.where(live_mask[None, :], logits, NEG_FILL)
        top_row = jnp.max(masked, axis=1)
        shifted = jnp.where(live_mask[None, :], masked - top_row[:, None], 0.0)
        expw = jnp.where(live_mask[None, :], jnp.exp(shifted), 0.0)
        target = jnp.sum(jnp.where(target_ids[:, None] == columns[None, :], logits, 0.0), axis=1)
        row_stats = jnp.stack([top_row, jnp.sum(expw, axis=1), jnp.sum(expw * shifted, axis=1), target])
        blocks = row_stats.reshape(4, seq_size, tok_rows).transpose(1, 0, 2)
    top_all, total_all, spread_all, target_all = merge_stats(blocks, kv_size, seq_size)
    log_probs = target_all - top_all - jnp.log(total_all)
    entropies = jnp.log(total_all) - spread_all / total_all
    return (log_probs, entropies)


def solution(mesh):
    in_specs = (
        P("seq", None),
        P(),
        P(None, "kv"),
        P(None, "kv"),
        P(None, "kv"),
        P("kv", None),
        P(),
        P(None, ("kv", "seq")),
        P(),
        P(),
        P(("kv", "seq")),
    )
    out_specs = (P("seq"), P("seq"))
    sizes = (mesh.shape["kv"], mesh.shape["seq"])
    return jax.shard_map(functools.partial(local, *sizes), mesh=mesh, in_specs=in_specs, out_specs=out_specs, check_vma=False)
```

```python
import functools
import math

import jax
import jax.numpy as jnp
from jax import lax
from jax.experimental import pallas as pl
from jax.experimental.pallas import tpu as pltpu
from jax.sharding import PartitionSpec as P

HEAD_DIM = 64


ROPE_THETA = 10000000.0
NORM_EPS = 1e-05
NEG_FILL = -1e30
ATTN_SCALE = 0.015625
RESID_SCALE = 5.0
LOGIT_SCALE = 0.125


def rms_norm(values, gain_vec):
    return (
        values * lax.rsqrt(jnp.mean(values * values, axis=-1, keepdims=True) + NORM_EPS) * gain_vec
    )


def rotate(values, positions):
    half_dim = values.shape[-1] // 2
    inverse = jnp.exp(
        jnp.arange(half_dim, dtype=jnp.float32) * (-2.0 * math.log(ROPE_THETA) / values.shape[-1])
    )
    angles = positions.astype(jnp.float32)[:, None] * inverse[None, :]
    cos_val = jnp.cos(angles)[:, None, :]
    sine_val = jnp.sin(angles)[:, None, :]
    lower_half = values[..., :half_dim]
    upper_half = values[..., half_dim:]
    return jnp.concatenate(
        [
            lower_half * cos_val - upper_half * sine_val,
            upper_half * cos_val + lower_half * sine_val,
        ],
        axis=-1,
    )


def enter(peers):
    barrier = pltpu.get_barrier_semaphore()
    for peer in peers:
        pl.semaphore_signal(barrier, inc=1, device_id=peer, device_id_type=pl.DeviceIdType.MESH)
    pl.semaphore_wait(barrier, len(peers))


def remote(src, dst, send_sem, recv_sem, peer):
    return pltpu.make_async_remote_copy(
        src_ref=src,
        dst_ref=dst,
        send_sem=send_sem,
        recv_sem=recv_sem,
        device_id=peer,
        device_id_type=pl.DeviceIdType.MESH,
    )


def seq_peer(kv_index, seq_index, step, seq_size):
    return {"kv": kv_index, "seq": lax.rem(seq_index + step, seq_size)}


def kv_peer(kv_index, seq_index, step, kv_size):
    return {"kv": lax.rem(kv_index + step, kv_size), "seq": seq_index}


def key_kernel(seq_size, reach, packed_ref, out_ref, local_sem, send_sem, recv_sem):
    kv_index, seq_index = lax.axis_index("kv"), lax.axis_index("seq")
    own = pltpu.make_async_copy(packed_ref, out_ref.at[reach], local_sem)
    own.start()
    enter([seq_peer(kv_index, seq_index, seq_size - d, seq_size) for d in range(1, reach + 1)])
    copies = []
    for d in range(1, reach + 1):
        copies.append(
            remote(
                packed_ref,
                out_ref.at[reach - d],
                send_sem.at[d - 1],
                recv_sem.at[d - 1],
                seq_peer(kv_index, seq_index, d, seq_size),
            )
        )
    for copy in copies:
        copy.start()
    own.wait()
    for copy in copies:
        copy.wait()


def gather_keys(packed, seq_size, reach):
    return pl.pallas_call(
        lambda *refs: key_kernel(seq_size, reach, *refs),
        out_shape=jax.ShapeDtypeStruct((reach + 1,) + packed.shape, packed.dtype),
        in_specs=[pl.BlockSpec(memory_space=pltpu.VMEM)],
        out_specs=pl.BlockSpec(memory_space=pltpu.VMEM),
        scratch_shapes=[
            pltpu.SemaphoreType.DMA,
            pltpu.SemaphoreType.DMA((reach,)),
            pltpu.SemaphoreType.DMA((reach,)),
        ],
        compiler_params=pltpu.CompilerParams(
            collective_id=0, has_side_effects=True, vmem_limit_bytes=40 * 2**20
        ),
    )(packed)


def block_plan(sizes, order):
    blocks = [(dict.fromkeys(order, 0), -1)]
    for level, dim in enumerate(order):
        fresh = []
        for place, _ in blocks:
            for step in range(1, sizes[dim]):
                fresh.append(({**place, dim: step}, level))
        blocks = blocks + fresh
    return blocks


def row_kernel(
    kv_size, seq_size, part_ref, hidden_ref, gain_ref, out_ref, heard, rs_send, rs_recv, send_sem, recv_sem
):
    kv_index, seq_index = lax.axis_index("kv"), lax.axis_index("seq")
    width = out_ref.shape[2]
    half = width // 2
    cores = 2 if kv_size % 2 == 0 else 1
    x_size = kv_size // cores
    y_size = x_size if seq_size % x_size == 0 else 1
    sizes = {"z": seq_size // y_size, "y": y_size, "x": x_size, "c": cores}
    mine = {
        "z": seq_index // y_size,
        "y": lax.rem(seq_index, y_size),
        "x": kv_index // cores,
        "c": lax.rem(kv_index, cores),
    }

    def at(place):
        now = {d: lax.rem(mine[d] + place[d], sizes[d]) if place[d] else mine[d] for d in sizes}
        return now["x"] * cores + now["c"], now["z"] * y_size + now["y"]

    def moved(dim, step):
        kv_at, seq_at = at({**dict.fromkeys(sizes, 0), dim: step})
        return {"kv": kv_at, "seq": seq_at}

    def slot(place):
        kv_at, seq_at = at(place)
        return seq_at * kv_size + kv_at

    peers = [kv_peer(kv_index, seq_index, step, kv_size) for step in range(1, kv_size)]
    peers += [moved(d, step) for d in ("z", "y") for step in range(1, sizes[d])]
    enter(peers)
    shares = []
    for step in range(1, kv_size):
        peer = kv_peer(kv_index, seq_index, step, kv_size)
        shares.append(
            remote(
                part_ref.at[peer["kv"]],
                heard.at[step - 1],
                rs_send.at[step - 1],
                rs_recv.at[step - 1],
                peer,
            )
        )
    for share in shares:
        share.start()
    total = part_ref[kv_index].astype(jnp.float32)
    for step, share in enumerate(shares):
        share.wait_recv()
        total = total + heard[step].astype(jnp.float32)
    values = hidden_ref[...].astype(jnp.float32) + RESID_SCALE * total
    out_ref[seq_index * kv_size + kv_index] = rms_norm(values, gain_ref[...]).astype(out_ref.dtype)

    orders = (("z", "y", "x", "c"), ("z", "x", "y", "c"))
    plans = [block_plan(sizes, order) for order in orders]
    sent = []
    used = [0, 0]
    for turn in range(kv_size * seq_size):
        for part in range(2):
            place, level = plans[part][turn]
            index = slot(place)
            view = out_ref.at[index, :, pl.ds(part * half, half)]
            if level >= 0:
                remote(
                    view, view, send_sem.at[part, 0], recv_sem.at[part, index], peers[0]
                ).wait_recv()
            for dim in orders[part][level + 1 :]:
                for step in range(1, sizes[dim]):
                    copy = remote(
                        view,
                        view,
                        send_sem.at[part, used[part]],
                        recv_sem.at[part, index],
                        moved(dim, step),
                    )
                    copy.start()
                    used[part] += 1
                    sent.append(copy)
    for copy in sent:
        copy.wait_send()
    for share in shares:
        share.wait_send()


def head_kernel(
    kv_size,
    seq_size,
    part_ref,
    hidden_ref,
    gain_ref,
    target_ref,
    live_ref,
    column_ref,
    head_ref,
    stat_ref,
    held,
    head,
    scored,
    heard,
    head_sem,
    rs_send,
    rs_recv,
    send_sem,
    recv_sem,
):
    kv_index, seq_index = lax.axis_index("kv"), lax.axis_index("seq")
    width = held.shape[2]
    half = width // 2
    rows = held.shape[1]
    weights = pltpu.make_async_copy(head_ref, head, head_sem)
    weights.start()
    cores = 2 if kv_size % 2 == 0 else 1
    x_size = kv_size // cores
    y_size = x_size if seq_size % x_size == 0 else 1
    sizes = {"z": seq_size // y_size, "y": y_size, "x": x_size, "c": cores}
    mine = {
        "z": seq_index // y_size,
        "y": lax.rem(seq_index, y_size),
        "x": kv_index // cores,
        "c": lax.rem(kv_index, cores),
    }

    def at(place):
        now = {d: lax.rem(mine[d] + place[d], sizes[d]) if place[d] else mine[d] for d in sizes}
        return now["x"] * cores + now["c"], now["z"] * y_size + now["y"]

    def moved(dim, step):
        kv_at, seq_at = at({**dict.fromkeys(sizes, 0), dim: step})
        return {"kv": kv_at, "seq": seq_at}

    def slot(place):
        kv_at, seq_at = at(place)
        column = (kv_at // cores) * y_size + lax.rem(seq_at, y_size)
        return (column * sizes["z"] + seq_at // y_size) * cores + lax.rem(kv_at, cores)

    peers = [kv_peer(kv_index, seq_index, step, kv_size) for step in range(1, kv_size)]
    peers += [moved(d, step) for d in ("z", "y") for step in range(1, sizes[d])]
    enter(peers)
    shares = []
    for step in range(1, kv_size):
        peer = kv_peer(kv_index, seq_index, step, kv_size)
        shares.append(
            remote(
                part_ref.at[peer["kv"]],
                heard.at[step - 1],
                rs_send.at[step - 1],
                rs_recv.at[step - 1],
                peer,
            )
        )
    for share in shares:
        share.start()
    total = part_ref[kv_index].astype(jnp.float32)
    for step, share in enumerate(shares):
        share.wait_recv()
        total = total + heard[step].astype(jnp.float32)
    values = hidden_ref[...].astype(jnp.float32) + RESID_SCALE * total
    held[slot(dict.fromkeys(sizes, 0))] = rms_norm(values, gain_ref[...]).astype(held.dtype)

    orders = (("z", "y", "x", "c"), ("z", "x", "y", "c"))
    sent = []
    used = [0, 0]

    def arrive(part, place):
        index = slot(place)
        view = held.at[index, :, pl.ds(part * half, half)]
        level = max([n for n, dim in enumerate(orders[part]) if place[dim]], default=-1)
        if level >= 0:
            remote(
                view, view, send_sem.at[part, 0], recv_sem.at[part, index], peers[0]
            ).wait_recv()
        for dim in orders[part][level + 1 :]:
            for step in range(1, sizes[dim]):
                copy = remote(
                    view,
                    view,
                    send_sem.at[part, used[part]],
                    recv_sem.at[part, index],
                    moved(dim, step),
                )
                copy.start()
                used[part] += 1
                sent.append(copy)

    depth = sizes["z"] * cores
    high = depth * rows
    total_columns = head.shape[0]
    cuts = [*range(0, total_columns - 511, 512)]
    tiles = list(zip(cuts, cuts[1:] + [total_columns])) if cuts else [(0, total_columns)]

    def score(x_step, y_step):
        first = slot({"z": 0, "y": y_step, "x": x_step, "c": 0}) // depth
        block = held[pl.ds(first * depth, depth)].reshape(high, width)
        wanted = jnp.broadcast_to(target_ref[first], (128, high)).T[:, 0:1]
        top = jnp.full((high, 1), NEG_FILL, jnp.float32)
        target = jnp.zeros((high, 1), jnp.float32)
        for low, end in tiles:
            logits = (
                lax.dot_general(
                    block,
                    head[low:end, :],
                    (((1,), (1,)), ((), ())),
                    preferred_element_type=jnp.float32,
                )
                * LOGIT_SCALE
            )
            masked = jnp.where(live_ref[:, low:end] == 1, logits, NEG_FILL)
            scored[:, low:end] = masked
            top = jnp.maximum(top, jnp.max(masked, axis=1, keepdims=True))
            hit = column_ref[:, low:end] == wanted
            target = target + jnp.sum(jnp.where(hit, logits, 0.0), axis=1, keepdims=True)
        total = jnp.zeros((high, 1), jnp.float32)
        spread = jnp.zeros((high, 1), jnp.float32)
        for low, end in tiles:
            shifted = scored[:, low:end] - top
            expw = jnp.exp(shifted)
            total = total + jnp.sum(expw, axis=1, keepdims=True)
            spread = spread + jnp.sum(expw * shifted, axis=1, keepdims=True)
        lane = lax.broadcasted_iota(jnp.int32, (high, 128), 1)
        table = jnp.where(lane == 0, top, jnp.where(lane == 1, total, jnp.where(lane == 2, spread, target)))
        stat_ref[first] = table.T[0:8]

    spots = [(i, j) for i in range(x_size) for j in range(y_size)]
    for stage in range(3):
        now = [spot for spot in spots if (spot[0] > 0) + (spot[1] > 0) == stage]
        for z_step in range(sizes["z"]):
            for i, j in now:
                for part in range(2):
                    arrive(part, {"z": z_step, "y": j, "x": i, "c": 0})
        if stage == 0:
            weights.wait()
        for i, j in now:
            for z_step in range(sizes["z"]):
                for c_step in range(1, cores):
                    for part in range(2):
                        arrive(part, {"z": z_step, "y": j, "x": i, "c": c_step})
            score(i, j)
    for copy in sent:
        copy.wait_send()
    for share in shares:
        share.wait_send()


def split_of(kv_size, seq_size):
    cores = 2 if kv_size % 2 == 0 else 1
    x_size = kv_size // cores
    y_size = x_size if seq_size % x_size == 0 else 1
    return seq_size // y_size, y_size, x_size, cores


def score_rows(part, hidden, gain, target_ids, live, columns, head, kv_size, seq_size):
    _, rows, width = part.shape
    count = kv_size * seq_size
    z_size, y_size, x_size, cores = split_of(kv_size, seq_size)
    spots = x_size * y_size
    high = z_size * cores * rows
    targets = target_ids.reshape(z_size, y_size, x_size, cores * rows)
    targets = targets.transpose(2, 1, 0, 3).reshape(spots, 1, high)
    stats = pl.pallas_call(
        lambda *refs: head_kernel(kv_size, seq_size, *refs),
        out_shape=jax.ShapeDtypeStruct((spots, 8, high), jnp.float32),
        in_specs=[pl.BlockSpec(memory_space=pltpu.VMEM)] * 6
        + [pl.BlockSpec(memory_space=pl.ANY)],
        out_specs=pl.BlockSpec(memory_space=pltpu.VMEM),
        scratch_shapes=[
            pltpu.VMEM((count, rows, width), jnp.bfloat16),
            pltpu.VMEM(head.shape, jnp.bfloat16),
            pltpu.VMEM((high, head.shape[0]), jnp.float32),
            pltpu.VMEM((kv_size - 1, rows, width), jnp.bfloat16),
            pltpu.SemaphoreType.DMA,
            pltpu.SemaphoreType.DMA((kv_size - 1,)),
            pltpu.SemaphoreType.DMA((kv_size - 1,)),
            pltpu.SemaphoreType.DMA((2, count)),
            pltpu.SemaphoreType.DMA((2, count)),
        ],
        compiler_params=pltpu.CompilerParams(
            collective_id=3, has_side_effects=True, vmem_limit_bytes=48 * 2**20
        ),
    )(part, hidden, gain, targets, live, columns, head)
    stats = stats[:, :4].reshape(x_size, y_size, 4, z_size, cores * rows)
    return stats.transpose(3, 1, 2, 0, 4).reshape(seq_size, 4, kv_size * rows)


def gather_rows(part, hidden, gain, kv_size, seq_size):
    _, rows, width = part.shape
    count = kv_size * seq_size
    return pl.pallas_call(
        lambda *refs: row_kernel(kv_size, seq_size, *refs),
        out_shape=jax.ShapeDtypeStruct((count, rows, width), jnp.bfloat16),
        in_specs=[pl.BlockSpec(memory_space=pltpu.VMEM)] * 3,
        out_specs=pl.BlockSpec(memory_space=pltpu.VMEM),
        scratch_shapes=[
            pltpu.VMEM((kv_size - 1, rows, width), jnp.bfloat16),
            pltpu.SemaphoreType.DMA((kv_size - 1,)),
            pltpu.SemaphoreType.DMA((kv_size - 1,)),
            pltpu.SemaphoreType.DMA((2, count)),
            pltpu.SemaphoreType.DMA((2, count)),
        ],
        compiler_params=pltpu.CompilerParams(
            collective_id=1, has_side_effects=True, vmem_limit_bytes=48 * 2**20
        ),
    )(part, hidden, gain)


def merge(stats):
    top = stats[0][0:1]
    for item in stats[1:]:
        top = jnp.maximum(top, item[0:1])
    total = spread = target = jnp.zeros_like(top)
    for item in stats:
        rescale = jnp.exp(item[0:1] - top)
        total = total + rescale * item[1:2]
        spread = spread + rescale * (item[2:3] + (item[0:1] - top) * item[1:2])
        target = target + item[3:4]
    return jnp.concatenate([top, total, spread, target], axis=0)


def stat_kernel(
    kv_size, seq_size, stat_ref, out_ref, near, block, far, send_one, recv_one, send_two, recv_two
):
    kv_index, seq_index = lax.axis_index("kv"), lax.axis_index("seq")
    by_seq = [seq_peer(kv_index, seq_index, step, seq_size) for step in range(1, seq_size)]
    by_kv = [kv_peer(kv_index, seq_index, step, kv_size) for step in range(1, kv_size)]
    enter(by_seq + by_kv)
    first = [
        remote(stat_ref.at[peer["seq"]], near.at[i], send_one.at[i], recv_one.at[i], peer)
        for i, peer in enumerate(by_seq)
    ]
    for copy in first:
        copy.start()
    for copy in first:
        copy.wait()
    block[...] = merge([stat_ref[seq_index]] + [near[i] for i in range(seq_size - 1)])
    second = [
        remote(block, far.at[i], send_two.at[i], recv_two.at[i], peer)
        for i, peer in enumerate(by_kv)
    ]
    for copy in second:
        copy.start()
    for copy in second:
        copy.wait()
    out_ref[...] = merge([block[...]] + [far[i] for i in range(kv_size - 1)])


def merge_stats(stats, kv_size, seq_size):
    one = stats.shape[1:]
    return pl.pallas_call(
        lambda *refs: stat_kernel(kv_size, seq_size, *refs),
        out_shape=jax.ShapeDtypeStruct(one, jnp.float32),
        in_specs=[pl.BlockSpec(memory_space=pltpu.VMEM)],
        out_specs=pl.BlockSpec(memory_space=pltpu.VMEM),
        scratch_shapes=[
            pltpu.VMEM((seq_size - 1,) + one, jnp.float32),
            pltpu.VMEM(one, jnp.float32),
            pltpu.VMEM((kv_size - 1,) + one, jnp.float32),
            pltpu.SemaphoreType.DMA((seq_size - 1,)),
            pltpu.SemaphoreType.DMA((seq_size - 1,)),
            pltpu.SemaphoreType.DMA((kv_size - 1,)),
            pltpu.SemaphoreType.DMA((kv_size - 1,)),
        ],
        compiler_params=pltpu.CompilerParams(
            collective_id=2, has_side_effects=True, vmem_limit_bytes=32 * 2**20
        ),
    )(stats)


def local(
    kv_size,
    seq_size,
    hidden_states,
    attn_gain,
    w_q,
    w_k,
    w_v,
    w_o,
    final_gain,
    w_head,
    doc_lengths,
    target_ids,
    vocab_mask,
):
    tok_rows = hidden_states.shape[0]
    seq_index = lax.axis_index("seq")
    kv_local = w_k.shape[1] // HEAD_DIM
    q_local = w_q.shape[1] // HEAD_DIM
    group_size = q_local // kv_local
    key_width = kv_local * HEAD_DIM
    stream = hidden_states.astype(jnp.float32)
    normed_in = rms_norm(stream, attn_gain).astype(jnp.bfloat16)
    queries = jnp.dot(normed_in, w_q, preferred_element_type=jnp.float32)
    key_proj = jnp.dot(normed_in, w_k, preferred_element_type=jnp.float32)
    value_proj = jnp.dot(normed_in, w_v, preferred_element_type=jnp.float32)
    token_pos = seq_index * tok_rows + jnp.arange(tok_rows, dtype=jnp.int32)
    docs = jnp.arange(doc_lengths.shape[0], dtype=jnp.int32)
    doc_starts = jnp.sum(jnp.where(docs[None, :] < docs[:, None], doc_lengths[None, :], 0), axis=1)
    doc_start = jnp.max(
        jnp.where(doc_starts[None, :] <= token_pos[:, None], doc_starts[None, :], 0), axis=1
    )
    positions = token_pos - doc_start
    rotated_q = rotate(queries.reshape(tok_rows, q_local, HEAD_DIM), positions).astype(jnp.bfloat16)
    rotated_q = rotated_q.reshape(tok_rows, kv_local, group_size, HEAD_DIM)
    rotated_k = rotate(key_proj.reshape(tok_rows, kv_local, HEAD_DIM), positions).astype(
        jnp.bfloat16
    )
    packed = jnp.concatenate(
        [rotated_k.reshape(tok_rows, key_width), value_proj.astype(jnp.bfloat16)], axis=1
    )
    reach = (seq_size + 1) // 2
    key_blocks = gather_keys(packed, seq_size, reach)
    row_count = (reach + 1) * tok_rows
    shard_rows = key_blocks.reshape(row_count, 2 * key_width)
    key_pos = (seq_index - reach) * tok_rows + jnp.arange(row_count, dtype=jnp.int32)
    key_rows = shard_rows[:, :key_width].reshape(row_count, kv_local, HEAD_DIM)
    value_rows = shard_rows[:, key_width:].reshape(row_count, kv_local, HEAD_DIM)
    scores = (
        jnp.einsum("tkgd,skd->kgts", rotated_q, key_rows, preferred_element_type=jnp.float32)
        * ATTN_SCALE
    )
    allowed = (key_pos[None, :] >= doc_start[:, None]) & (key_pos[None, :] <= token_pos[:, None])
    scores = jnp.where(allowed, scores, NEG_FILL)
    top_score = jnp.max(scores, axis=-1)
    weights = jnp.where(allowed, jnp.exp(scores - top_score[..., None]), 0.0)
    totals = jnp.sum(weights, axis=-1)
    context_sum = jnp.einsum(
        "kgts,skd->kgtd",
        weights.astype(jnp.bfloat16),
        value_rows,
        preferred_element_type=jnp.float32,
    )
    context = (
        (context_sum / totals[..., None])
        .transpose(2, 0, 1, 3)
        .reshape(tok_rows, q_local * HEAD_DIM)
        .astype(jnp.bfloat16)
    )
    vocab_local = w_head.shape[1]
    flat_rank = lax.axis_index(("kv", "seq"))
    live_mask = vocab_mask == 1
    columns = flat_rank * vocab_local + jnp.arange(vocab_local, dtype=jnp.int32)
    own_rows = tok_rows // kv_size
    part = jnp.dot(context, w_o, preferred_element_type=jnp.float32).astype(jnp.bfloat16)
    own_hidden = lax.dynamic_slice_in_dim(
        hidden_states, lax.axis_index("kv") * own_rows, own_rows, 0
    )
    if own_rows % 16 == 0:
        blocks = score_rows(
            part.reshape(kv_size, own_rows, part.shape[1]),
            own_hidden,
            final_gain[None, :],
            target_ids,
            vocab_mask[None, :],
            columns[None, :],
            w_head.T,
            kv_size,
            seq_size,
        )
    else:
        head_shard_rows = gather_rows(
            part.reshape(kv_size, own_rows, part.shape[1]),
            own_hidden,
            final_gain[None, :],
            kv_size,
            seq_size,
        ).reshape(tok_rows * seq_size, part.shape[1])
        logits = jnp.dot(head_shard_rows, w_head, preferred_element_type=jnp.float32) * LOGIT_SCALE
        masked = jnp.where(live_mask[None, :], logits, NEG_FILL)
        top_row = jnp.max(masked, axis=1)
        shifted = jnp.where(live_mask[None, :], masked - top_row[:, None], 0.0)
        expw = jnp.where(live_mask[None, :], jnp.exp(shifted), 0.0)
        target = jnp.sum(jnp.where(target_ids[:, None] == columns[None, :], logits, 0.0), axis=1)
        row_stats = jnp.stack([top_row, jnp.sum(expw, axis=1), jnp.sum(expw * shifted, axis=1), target])
        blocks = row_stats.reshape(4, seq_size, tok_rows).transpose(1, 0, 2)
    top_all, total_all, spread_all, target_all = merge_stats(blocks, kv_size, seq_size)
    log_probs = target_all - top_all - jnp.log(total_all)
    entropies = jnp.log(total_all) - spread_all / total_all
    return (log_probs, entropies)


def solution(mesh):
    in_specs = (
        P("seq", None),
        P(),
        P(None, "kv"),
        P(None, "kv"),
        P(None, "kv"),
        P("kv", None),
        P(),
        P(None, ("kv", "seq")),
        P(),
        P(),
        P(("kv", "seq")),
    )
    out_specs = (P("seq"), P("seq"))
    sizes = (mesh.shape["kv"], mesh.shape["seq"])
    return jax.shard_map(functools.partial(local, *sizes), mesh=mesh, in_specs=in_specs, out_specs=out_specs, check_vma=False)
```
